256 devices in a mesh: row: 64 (over y, z, core), col: 4 (over x).
Axes of the slice: x: 4, y: 4, z: 8, core: 2. Of those that a mesh axis runs over, the one named last changes fastest.
Arguments:
- diag_block: float32 [1024, 1024], P('row', 'col'), may hold values from -3 to 3, as said below
- block_rhs: float32 [1024, 512], P('row', 'col'), may hold values from -6 to 6
- panel: float32 [262144, 1024], P('row', 'col'), may hold values from -0.1875 to 0.1875
- trailing_rhs: float32 [262144, 512], P('row', 'col'), may hold values from -6 to 6
Outputs:
- solved: float32 [1024, 512], P('row', 'col')
- trailing: float32 [262144, 512], P('row', 'col')
The draws below stay inside these ranges and needn't reach their ends.
Inputs may be any that keep to these rules, and one draw needn't show every extreme that they name: diag_block is zero above its diagonal; its diagonal entries lie between 1.5 and 3.
All inputs are finite; a program needn't handle non-finite values.
Results may differ from the reference program's by a relative error of at most 0.000096.
Values sent between devices are 32-bit elements; how exact they have to be, the bound alone decides.
No kernel may reach another device: no remote copies, remote signals or barrier semaphores. Data moves between devices by JAX's collectives and lax.ppermute only.
A program may use at most 128 MiB of HBM per device.

```python
import jax
import jax.numpy as jnp
from jax import lax

NB = 1024
NRHS = 512
PANEL = 262144


def draw_diag_block(key, part):
    key = jax.random.fold_in(key, 7)
    first_key, second_key = jax.random.split(key)
    spread_factor = 0.6 * NB ** (-0.5)
    lower_part = jnp.clip(jax.random.normal(first_key, (NB, NB), jnp.float32), -4.0, 4.0) * spread_factor
    diagonal = jax.random.uniform(second_key, (NB,), jnp.float32, 1.5, 3.0)
    return jnp.tril(lower_part, -1) + jnp.diag(diagonal)


def shard_levels(own_key, shape, pieces, low, largest):
    level = 1.0
    for dim, parts in pieces:
        heights = jax.random.uniform(jax.random.fold_in(jax.random.fold_in(own_key, 6), dim), (parts,), jnp.float32, low / len(pieces), largest / len(pieces))
        level = level * jnp.repeat(jnp.exp(heights), shape[dim] // parts).reshape((-1,) + (1,) * (len(shape) - 1 - dim))
    return level


def scatter_about(key, extent, width, most, cuts=(), dtype=jnp.bfloat16):
    factor_of = shard_levels(key, extent, cuts, -0.22, 0.18) if cuts else 1.0
    array = jax.random.normal(key, extent, jnp.float32) * width * factor_of
    return jnp.minimum(jnp.maximum(array, -most), most).astype(dtype)


def setup_inputs(seed: int = 0) -> dict:
    arg_keys = jax.random.split(jax.random.key(seed), 5)
    diag_block = draw_diag_block(jax.random.fold_in(arg_keys[4], 71), 0)
    block_rhs = scatter_about(arg_keys[1], (NB, NRHS), 1.0, 6.0, ((0, 64), (1, 4)), jnp.float32)
    panel = scatter_about(arg_keys[2], (PANEL, NB), NB ** -0.5, 0.1875, ((0, 64), (1, 4)), jnp.float32)
    trailing_rhs = scatter_about(arg_keys[3], (PANEL, NRHS), 1.0, 6.0, ((0, 64), (1, 4)), jnp.float32)
    return {"diag_block": diag_block, "block_rhs": block_rhs, "panel": panel, "trailing_rhs": trailing_rhs}


def reference(diag_block, block_rhs, panel, trailing_rhs):
    solved = lax.linalg.triangular_solve(diag_block, block_rhs, left_side=True, lower=True)
    product = jnp.dot(panel.astype(jnp.float32), solved.astype(jnp.float32), preferred_element_type=jnp.float32, precision=lax.Precision.HIGHEST)
    trailing = trailing_rhs - product
    return (solved, trailing)
```

```python
import jax
import jax.numpy as jnp
from jax import lax
from jax.experimental import pallas as pl
from jax.experimental.pallas import tpu as pltpu
from jax.sharding import PartitionSpec as P

NY, NZ, NC = 4, 8, 2
HALVES = 2
MIB = 1024 * 1024


def mm(a, b):
    return jnp.dot(a, b, preferred_element_type=jnp.float32, precision=lax.Precision.HIGHEST)


def tiny_inverses(blocks):
    n = len(blocks)
    lane = lax.broadcasted_iota(jnp.int32, (16, 128), 1)
    row = lax.broadcasted_iota(jnp.int32, (16, 128), 0)
    seg = lane // 16
    packed = []
    for a in blocks:
        p = jnp.zeros((16, 128), jnp.float32)
        for s in range(8):
            p = jnp.where(seg == s, a[16 * s : 16 * s + 16, :], p)
        packed.append(p)
    p = jnp.concatenate(packed, axis=0)
    lane_n = lax.broadcasted_iota(jnp.int32, (16 * n, 128), 1)
    r = jnp.where(lane == seg * 16 + row, 1.0, 0.0).astype(jnp.float32)
    r = jnp.broadcast_to(r[None], (n, 16, 128))
    row3 = lax.broadcasted_iota(jnp.int32, (n, 16, 128), 1)
    for j in range(16):
        idx = (lane_n // 16) * 16 + j
        column = jnp.take_along_axis(p, idx, axis=1).reshape(n, 16, 128)
        w = r[:, j : j + 1, :] / column[:, j : j + 1, :]
        r = jnp.where(row3 > j, r - column * w, jnp.where(row3 == j, w, r))
    return [
        jnp.concatenate([jnp.where(seg == s, r[b], 0.0) for s in range(8)], axis=0) for b in range(n)
    ]


def grow(a, d, s):
    i = lax.broadcasted_iota(jnp.int32, a.shape, 0)
    k = lax.broadcasted_iota(jnp.int32, a.shape, 1)
    off = (i // (2 * s) == k // (2 * s)) & ((i // s) % 2 == 1) & ((k // s) % 2 == 0)
    return d - mm(d, mm(jnp.where(off, a, 0.0), d))


BELOW = ((1, 0), (2, 0), (2, 1), (3, 0), (3, 1), (3, 2))


def split(a):
    high = a.astype(jnp.bfloat16)
    return high, (a - high.astype(jnp.float32)).astype(jnp.bfloat16)


def solve_kernel(where, low_own, low_other, *refs):
    own4, other4, (x_ref, xh, xl, dinv, rest) = refs[:4], refs[4:8], refs[8:]
    first = where[0] == 0

    def rows(own, other):
        a = jnp.where(first, own, other)
        b = jnp.where(first, other, own)
        return jnp.stack([a, b], axis=1).reshape(256, own.shape[-1])

    def lower(k, j):
        n = BELOW.index((k, j))
        return rows(low_own[:, n], low_other[:, n])

    for n in range(NY):
        rest[(where[1] + n) % NY] = rows(own4[n][...], other4[n][...])

    def diagonal(k):
        return rest[k, :, :256]

    blocks = []
    for k in range(NY):
        t = diagonal(k)
        blocks += [t[:128, :128], t[128:, 128:]]
    ds = tiny_inverses(blocks)
    for s in (16, 32, 64):
        ds = [grow(a, d, s) for a, d in zip(blocks, ds)]
    for k in range(NY):
        da, db = ds[2 * k], ds[2 * k + 1]
        dinv[k, :128, :128] = da
        dinv[k, :128, 128:] = jnp.zeros((128, 128), jnp.float32)
        dinv[k, 128:, :128] = -mm(db, mm(diagonal(k)[128:, :128], da))
        dinv[k, 128:, 128:] = db
    for k in range(NY):
        r = rest[k, :, 256:]
        for j in range(k):
            r = r - mm(lower(k, j), x_ref[256 * j : 256 * j + 256, :])
        x = mm(dinv[k], r)
        x_ref[256 * k : 256 * k + 256, :] = x
        xh[k], xl[k] = split(x)


def solve(where, low_own, low_other, rests, rests_other):
    vmem = pl.BlockSpec(memory_space=pltpu.VMEM)
    return pl.pallas_call(
        solve_kernel,
        out_shape=[jax.ShapeDtypeStruct((1024, 512), jnp.float32)]
        + [jax.ShapeDtypeStruct((NY, 256, 512), jnp.bfloat16)] * 2,
        in_specs=[pl.BlockSpec(memory_space=pltpu.SMEM)] + [vmem] * 10,
        out_specs=[vmem] * 3,
        scratch_shapes=[pltpu.VMEM((NY, 256, 256), jnp.float32), pltpu.VMEM((NY, 256, 768), jnp.float32)],
        compiler_params=pltpu.CompilerParams(vmem_limit_bytes=12 * MIB),
        cost_estimate=pl.CostEstimate(flops=4 * 10**9, bytes_accessed=8 * MIB, transcendentals=0),
    )(where, low_own, low_other, *rests, *rests_other)


def product_kernel(col_ref, own, left, right, far, xh, xl, *refs):
    outs, parts = refs[:4], refs[4]
    acc = jnp.zeros((own.shape[0], 512), jnp.float32)
    for piece, shift in ((own, 0), (left, 3), (right, 1), (far, 2)):
        k = (col_ref[0] + shift) % 4
        ah, al = split(piece[...])
        bh, bl = xh[k], xl[k]
        for a, b in ((ah, bh), (ah, bl), (al, bh)):
            acc += jnp.dot(a, b, preferred_element_type=jnp.float32)
    for j in range(4):
        parts[j] = acc[:, 128 * j : 128 * j + 128]
    for k in range(4):
        outs[k][...] = parts[(col_ref[0] + k) % 4]


def product(col, panel, half, pieces, xh, xl):
    n, tile = pieces[0].shape[0], 256
    steps = n // tile
    piece = pl.BlockSpec((tile, 256), lambda i, c: (i, 0))
    full = pl.BlockSpec((4, 256, 512), lambda i, c: (0, 0, 0))
    out = pl.BlockSpec((tile, 128), lambda i, c: (i, 0))
    return pl.pallas_call(
        product_kernel,
        out_shape=[jax.ShapeDtypeStruct((n, 128), jnp.float32)] * 4,
        grid_spec=pltpu.PrefetchScalarGridSpec(
            num_scalar_prefetch=1,
            grid=(steps,),
            in_specs=[pl.BlockSpec((tile, 256), lambda i, c: ((c[0] * HALVES + half) * steps + i, 0))]
            + [piece] * 3
            + [full] * 2,
            out_specs=[out] * 4,
            scratch_shapes=[pltpu.VMEM((4, tile, 128), jnp.float32)],
        ),
        compiler_params=pltpu.CompilerParams(vmem_limit_bytes=16 * MIB),
        cost_estimate=pl.CostEstimate(flops=6 * n * 1024 * 512, bytes_accessed=6 * MIB, transcendentals=0),
    )(col, panel, *pieces, xh, xl)


def finish_kernel(col_ref, rhs, own, left, right, far, *refs):
    out = refs[-1]
    for n, piece in enumerate((own, left, right, far)):

        @pl.when(pl.program_id(0) == n)
        def _():
            out[...] = rhs[...] - piece[...]


def finish(col, rhs, half, pieces, before):
    n = pieces[0].shape[0]

    def block(i, c):
        source = (c[0] + jnp.where(i == 0, 0, jnp.where(i == 1, 3, i - 1))) % 4
        return (source * HALVES + half, 0)

    piece = pl.BlockSpec((n, 128), lambda i, c: (0, 0))
    prior = [] if before is None else [before]
    return pl.pallas_call(
        finish_kernel,
        out_shape=jax.ShapeDtypeStruct(rhs.shape, jnp.float32),
        grid_spec=pltpu.PrefetchScalarGridSpec(
            num_scalar_prefetch=1,
            grid=(4,),
            in_specs=[pl.BlockSpec((n, 128), block)] + [piece] * 4 + [pl.BlockSpec(memory_space=pl.ANY)] * len(prior),
            out_specs=pl.BlockSpec((n, 128), block),
        ),
        input_output_aliases={6: 0} if prior else {},
        compiler_params=pltpu.CompilerParams(vmem_limit_bytes=16 * MIB),
        cost_estimate=pl.CostEstimate(flops=4 * n * 128, bytes_accessed=12 * n * 512, transcendentals=0),
    )(col, rhs, *pieces, *prior)


def z_groups():
    return [[(y * NZ + z) * NC + c for z in range(NZ)] for y in range(NY) for c in range(NC)]


def y_groups():
    return [[(y * NZ + z) * NC + c for y in range(NY)] for z in range(NZ) for c in range(NC)]


def spread(a, axis, n, groups=None):
    return lax.all_to_all(
        jnp.broadcast_to(a[None], (n,) + a.shape), axis, 0, 0, tiled=True, axis_index_groups=groups
    )


def swap_cores(a):
    return lax.ppermute(a, "row", [(i, i ^ 1) for i in range(NY * NZ * NC)])


def shift_y(a, k):
    step = k * NZ * NC
    n = NY * NZ * NC
    return lax.ppermute(a, "row", [(i, (i + step) % n) for i in range(n)])


def send_x(a, k):
    return lax.ppermute(a, "col", [(i, (i + k) % 4) for i in range(4)])


def from_planes(a, y):
    parts = jnp.stack([a, shift_y(a, 3), shift_y(a, 2), shift_y(a, 1)])
    return [lax.dynamic_index_in_dim(parts, (k - y) % NY, 0, keepdims=False) for k in range(NY)]


def per_device(diag_block, block_rhs, panel, trailing_rhs):
    row, col = lax.axis_index("row"), lax.axis_index("col")
    y = row // (NZ * NC)
    quarter = panel.shape[0] // 4

    mine = spread(jnp.concatenate([diag_block, block_rhs], axis=1), "col", 4)
    chunk = panel.shape[0] // (4 * HALVES)
    chunks = [
        [lax.dynamic_slice_in_dim(panel, ((col + k) % 4 * HALVES + h) * chunk, chunk, 0) for k in (1, 3, 2)]
        for h in range(HALVES)
    ]
    mine, chunks = lax.optimization_barrier((mine, chunks))
    moved = [[send_x(p, k) for p, k in zip(c, (1, 3, 2))] for c in chunks]

    diagonal = lax.dynamic_index_in_dim(mine, y, 0, keepdims=False)[:, :256]
    rest = jnp.concatenate([diagonal] + [mine[c, :, 256:] for c in range(4)], axis=1)
    rest = spread(rest, "row", NZ, z_groups())
    low = from_planes(mine[:3, :, :256], y)
    low = jnp.stack([low[k][j] for k, j in BELOW])
    moved[0], rest, low = lax.optimization_barrier((moved[0], rest, low))
    low = spread(low, "row", NZ, z_groups())
    others = [shift_y(rest, k) for k in (3, 2, 1)]
    moved[1], low, others = lax.optimization_barrier((moved[1], low, others))
    rests = [rest] + others
    low_other, rests_other = swap_cores(low), [swap_cores(r) for r in rests]
    where = jnp.stack([row % NC, y]).astype(jnp.int32)
    x, xh, xl = solve(where, low, low_other, rests, rests_other)

    me = jnp.reshape(col, (1,)).astype(jnp.int32)
    parts = [product(me, panel, h, moved[h], xh, xl) for h in range(HALVES)]
    trailing = None
    for h in range(HALVES):
        own, *sent = parts[h]
        far = send_x(sent[1], 2)
        pieces = [own, send_x(sent[0], 1), send_x(sent[2], 3), far]
        trailing = finish(me, trailing_rhs, h, pieces, trailing)
    stripe = lax.dynamic_slice(x, (row * block_rhs.shape[0], col * 128), block_rhs.shape)
    return (stripe, trailing)


def solution(mesh):
    specs = (P("row", "col"),) * 4
    return jax.shard_map(per_device, mesh=mesh, in_specs=specs, out_specs=(P("row", "col"),) * 2, check_vma=False)
```

```python
import functools

import jax
import jax.numpy as jnp
from jax import lax
from jax.experimental import pallas as pl
from jax.experimental.pallas import tpu as pltpu
from jax.sharding import PartitionSpec as P

NY, NZ, NC = 4, 8, 2
MIB = 1024 * 1024


def mm(a, b):
    return jnp.dot(a, b, preferred_element_type=jnp.float32, precision=lax.Precision.HIGHEST)


def tiny_inverses(blocks):
    n = len(blocks)
    lane = lax.broadcasted_iota(jnp.int32, (16, 128), 1)
    row = lax.broadcasted_iota(jnp.int32, (16, 128), 0)
    seg = lane // 16
    packed = []
    for a in blocks:
        p = jnp.zeros((16, 128), jnp.float32)
        for s in range(8):
            p = jnp.where(seg == s, a[16 * s : 16 * s + 16, :], p)
        packed.append(p)
    p = jnp.concatenate(packed, axis=0)
    lane_n = lax.broadcasted_iota(jnp.int32, (16 * n, 128), 1)
    r = jnp.where(lane == seg * 16 + row, 1.0, 0.0).astype(jnp.float32)
    r = jnp.broadcast_to(r[None], (n, 16, 128))
    row3 = lax.broadcasted_iota(jnp.int32, (n, 16, 128), 1)
    for j in range(16):
        idx = (lane_n // 16) * 16 + j
        column = jnp.take_along_axis(p, idx, axis=1).reshape(n, 16, 128)
        w = r[:, j : j + 1, :] / column[:, j : j + 1, :]
        r = jnp.where(row3 > j, r - column * w, jnp.where(row3 == j, w, r))
    return [
        jnp.concatenate([jnp.where(seg == s, r[b], 0.0) for s in range(8)], axis=0) for b in range(n)
    ]


def grow(a, d, s):
    i = lax.broadcasted_iota(jnp.int32, a.shape, 0)
    k = lax.broadcasted_iota(jnp.int32, a.shape, 1)
    off = (i // (2 * s) == k // (2 * s)) & ((i // s) % 2 == 1) & ((k // s) % 2 == 0)
    return d - mm(d, mm(jnp.where(off, a, 0.0), d))


BELOW = ((1, 0), (2, 0), (2, 1), (3, 0), (3, 1), (3, 2))


def split(a):
    high = a.astype(jnp.bfloat16)
    return high, (a - high.astype(jnp.float32)).astype(jnp.bfloat16)


def weave(first, own, other):
    a, b = jnp.where(first, own, other), jnp.where(first, other, own)
    return jnp.stack([a, b], axis=1).reshape(256, own.shape[-1])


def prepare_kernel(where, *refs):
    own4, other4, (result, mark, out, sems) = refs[:4], refs[4:8], refs[8:]
    first = where[0] == 0
    for n in range(NY):
        out[(where[1] + n) % NY] = weave(first, own4[n][...], other4[n][...])
    blocks = []
    for k in range(NY):
        blocks += [out[k, :128, :128], out[k, 128:, 128:256]]
    ds = tiny_inverses(blocks)
    for s in (16, 32, 64):
        ds = [grow(a, d, s) for a, d in zip(blocks, ds)]
    lows = [mm(ds[2 * k + 1], mm(out[k, 128:, :128], ds[2 * k])) for k in range(NY)]
    for k in range(NY):
        out[k, :128, :128] = ds[2 * k]
        out[k, :128, 128:256] = jnp.zeros((128, 128), jnp.float32)
        out[k, 128:, :128] = -lows[k]
        out[k, 128:, 128:256] = ds[2 * k + 1]
        out[k, :, 256:] = mm(out[k, :, :256], out[k, :, 256:])
        pltpu.make_async_copy(out.at[k], result.at[k], sems.at[k]).start()
    mark[...] = out[NY - 1, :8, :128]
    for k in range(NY):
        pltpu.make_async_copy(out.at[k], result.at[k], sems.at[k]).wait()


def prepare(where, own, other):
    vmem = pl.BlockSpec(memory_space=pltpu.VMEM)
    return pl.pallas_call(
        prepare_kernel,
        out_shape=[pltpu.HBM((NY, 256, 768), jnp.float32), jax.ShapeDtypeStruct((8, 128), jnp.float32)],
        in_specs=[pl.BlockSpec(memory_space=pltpu.SMEM)] + [vmem] * 8,
        out_specs=[pl.BlockSpec(memory_space=pltpu.HBM), vmem],
        scratch_shapes=[pltpu.VMEM((NY, 256, 768), jnp.float32), pltpu.SemaphoreType.DMA((NY,))],
        compiler_params=pltpu.CompilerParams(vmem_limit_bytes=16 * MIB),
        cost_estimate=pl.CostEstimate(flops=10 * 10**9, bytes_accessed=8 * MIB, transcendentals=0),
    )(where, *own, *other)


def solve_kernel(where, low_own, low_other, prepared, mark, stripe, xh, xl, x_ref, ready, sems):
    first = where[0] == 0
    fetches = [pltpu.make_async_copy(prepared.at[k], ready.at[k], sems.at[k]) for k in range(NY)]
    for fetch in fetches:
        fetch.start()
    for k in range(NY):
        fetches[k].wait()
        x = ready[k, :, 256:]
        if k > 0:
            total = jnp.zeros((256, 512), jnp.float32)
            for j in range(k):
                n = BELOW.index((k, j))
                total += mm(weave(first, low_own[:, n], low_other[:, n]), x_ref[256 * j : 256 * j + 256, :])
            x = x - mm(ready[k, :, :256], total)
        x_ref[256 * k : 256 * k + 256, :] = x
        slot = pl.ds(pl.multiple_of((k + 4 - where[4]) % 4 * 256, 256), 256)
        xh[slot, :], xl[slot, :] = split(x)
    stripe[...] = x_ref[pl.ds(pl.multiple_of(where[2], 16), 16), pl.ds(pl.multiple_of(where[3], 128), 128)]


def solve(where, low_own, low_other, ready, mark):
    vmem = pl.BlockSpec(memory_space=pltpu.VMEM)
    return pl.pallas_call(
        solve_kernel,
        out_shape=[jax.ShapeDtypeStruct((16, 128), jnp.float32)] + [jax.ShapeDtypeStruct((1024, 512), jnp.bfloat16)] * 2,
        in_specs=[pl.BlockSpec(memory_space=pltpu.SMEM), vmem, vmem, pl.BlockSpec(memory_space=pltpu.HBM), vmem],
        out_specs=[vmem] * 3,
        scratch_shapes=[
            pltpu.VMEM((1024, 512), jnp.float32),
            pltpu.VMEM((NY, 256, 768), jnp.float32),
            pltpu.SemaphoreType.DMA((NY,)),
        ],
        compiler_params=pltpu.CompilerParams(vmem_limit_bytes=14 * MIB),
        cost_estimate=pl.CostEstimate(flops=4 * 10**9, bytes_accessed=8 * MIB, transcendentals=0),
    )(where, low_own, low_other, ready, mark)


def product_kernel(col_ref, own, right, far, left, xh, xl, *refs):
    outs, parts = refs[:4], refs[4]
    ah, al = split(jnp.concatenate([own[...], right[...], far[...], left[...]], axis=1))
    acc = jnp.dot(ah, xh[...], preferred_element_type=jnp.float32)
    acc += jnp.dot(ah, xl[...], preferred_element_type=jnp.float32)
    acc += jnp.dot(al, xh[...], preferred_element_type=jnp.float32)
    for j in range(4):
        parts[j] = acc[:, 128 * j : 128 * j + 128]
    for k in range(4):
        outs[k][...] = parts[(col_ref[0] + k) % 4]


def product(col, pieces, xh, xl):
    n, tile = pieces[0].shape[0], 256
    piece = pl.BlockSpec((tile, 256), lambda i, c: (i, 0))
    full = pl.BlockSpec((1024, 512), lambda i, c: (0, 0))
    return pl.pallas_call(
        product_kernel,
        out_shape=[jax.ShapeDtypeStruct((n, 128), jnp.float32)] * 4,
        grid_spec=pltpu.PrefetchScalarGridSpec(
            num_scalar_prefetch=1,
            grid=(n // tile,),
            in_specs=[piece] * 4 + [full] * 2,
            out_specs=[pl.BlockSpec((tile, 128), lambda i, c: (i, 0))] * 4,
            scratch_shapes=[pltpu.VMEM((4, tile, 128), jnp.float32)],
        ),
        compiler_params=pltpu.CompilerParams(vmem_limit_bytes=14 * MIB),
        cost_estimate=pl.CostEstimate(flops=6 * n * 1024 * 512, bytes_accessed=6 * MIB, transcendentals=0),
    )(col, *pieces, xh, xl)


def finish_kernel(source_ref, rhs, piece, *refs):
    refs[-1][...] = rhs[...] - piece[...]


def finish(source, rhs, piece, before):
    n, steps = piece.shape[0], 1
    tile = n // steps
    block = pl.BlockSpec((tile, 128), lambda i, s: (s[0] * steps + i, 0))
    prior = [] if before is None else [before]
    return pl.pallas_call(
        finish_kernel,
        out_shape=jax.ShapeDtypeStruct(rhs.shape, jnp.float32),
        grid_spec=pltpu.PrefetchScalarGridSpec(
            num_scalar_prefetch=1,
            grid=(steps,),
            in_specs=[block, pl.BlockSpec((tile, 128), lambda i, s: (i, 0))]
            + [pl.BlockSpec(memory_space=pl.ANY)] * len(prior),
            out_specs=block,
        ),
        input_output_aliases={3: 0} if prior else {},
        compiler_params=pltpu.CompilerParams(vmem_limit_bytes=16 * MIB),
        cost_estimate=pl.CostEstimate(flops=n * 128, bytes_accessed=3 * n * 512, transcendentals=0),
    )(source, rhs, piece, *prior)


def copies_kernel(fill, n, *refs):
    out = refs[-1]
    fill(*refs)
    for i in range(1, n):
        out[i] = out[0]


def copies(fill, n, shape, *args):
    vmem = pl.BlockSpec(memory_space=pltpu.VMEM)
    inputs = pl.BlockSpec() if fill is fill_mine else vmem
    specs = [pl.BlockSpec(memory_space=pltpu.SMEM) if a.dtype == jnp.int32 else inputs for a in args]
    return pl.pallas_call(
        functools.partial(copies_kernel, fill, n),
        out_shape=jax.ShapeDtypeStruct((n,) + shape, jnp.float32),
        in_specs=specs,
        out_specs=vmem,
        compiler_params=pltpu.CompilerParams(vmem_limit_bytes=8 * MIB),
        cost_estimate=pl.CostEstimate(flops=0, bytes_accessed=MIB, transcendentals=0),
    )(*args)


def fill_mine(diag, rhs, out):
    out[0, :, :256] = diag[...]
    out[0, :, 256:] = rhs[...]


def fill_rest(where, mine, out):
    out[0, :, :256] = mine[where[1], :, :256]
    for c in range(4):
        out[0, :, 256 + 128 * c : 384 + 128 * c] = mine[c, :, 256:]


def fill_low(where, mine, *refs):
    out = refs[3]
    for n, (k, j) in enumerate(BELOW):
        step = (k - where[1] + NY) % NY
        part = mine[j, :, :256]
        for m in range(3):
            part = jnp.where(step == m + 1, refs[m][j], part)
        out[0, n] = part


def z_groups():
    return [[(y * NZ + z) * NC + c for z in range(NZ)] for y in range(NY) for c in range(NC)]


def y_groups():
    return [[(y * NZ + z) * NC + c for y in range(NY)] for z in range(NZ) for c in range(NC)]


def send_copies(a, axis, groups=None):
    return lax.all_to_all(a, axis, 0, 0, tiled=True, axis_index_groups=groups)


def swap_cores(a):
    return lax.ppermute(a, "row", [(i, i ^ 1) for i in range(NY * NZ * NC)])


def shift_y(a, k):
    step = k * NZ * NC
    n = NY * NZ * NC
    return lax.ppermute(a, "row", [(i, (i + step) % n) for i in range(n)])


def send_x(a, k):
    return lax.ppermute(a, "col", [(i, (i + k) % 4) for i in range(4)])


def per_device(diag_block, block_rhs, panel, trailing_rhs):
    row, col = lax.axis_index("row"), lax.axis_index("col")
    y = row // (NZ * NC)
    where = jnp.stack([row % NC, y, row * 16, col * 128, col]).astype(jnp.int32)

    mine = send_copies(copies(fill_mine, 4, (16, 384), *[pltpu.with_memory_space_constraint(a, pltpu.HBM) for a in (diag_block, block_rhs)]), "col")
    quarter = panel.shape[0] // 4
    own, *pieces = [lax.dynamic_slice_in_dim(panel, (col + k) % 4 * quarter, quarter, 0) for k in (0, 2, 1, 3)]
    mine, pieces = lax.optimization_barrier((mine, pieces))
    far, left, right = [send_x(p, k) for k, p in zip((2, 1, 3), pieces)]

    rest = send_copies(copies(fill_rest, NZ, (16, 768), where, mine), "row", z_groups())
    lows = [shift_y(mine[:3, :, :256], k) for k in (3, 2, 1)]
    rest, lows = lax.optimization_barrier((rest, lows))
    low = send_copies(copies(fill_low, NZ, (6, 16, 256), where, mine, *lows), "row", z_groups())
    rests = [rest] + [shift_y(rest, k) for k in (3, 2, 1)]
    far, left, right, rests = lax.optimization_barrier((far, left, right, rests))
    ready, mark = prepare(where, rests, [swap_cores(r) for r in rests])
    low, mark = lax.optimization_barrier((low, mark))
    stripe, xh, xl = solve(where, low, swap_cores(low), pltpu.with_memory_space_constraint(ready, pltpu.HBM), mark)

    def source(k):
        return jnp.reshape((col + k) % 4, (1,)).astype(jnp.int32)

    mine, to_right, to_far, to_left = product(source(0), (own, right, far, left), xh, xl)
    got_far, got_left, got_right = send_x(to_far, 2), send_x(to_right, 1), send_x(to_left, 3)
    trailing = finish(source(0), trailing_rhs, mine, None)
    trailing = finish(source(2), trailing_rhs, got_far, trailing)
    trailing = finish(source(3), trailing_rhs, got_left, trailing)
    trailing = finish(source(1), trailing_rhs, got_right, trailing)
    return (stripe, trailing)


def solution(mesh):
    specs = (P("row", "col"),) * 4
    return jax.shard_map(per_device, mesh=mesh, in_specs=specs, out_specs=(P("row", "col"),) * 2, check_vma=False)
```

```python
import functools

import jax
import jax.numpy as jnp
from jax import lax
from jax.experimental import pallas as pl
from jax.experimental.pallas import tpu as pltpu
from jax.sharding import PartitionSpec as P

NY, NZ, NC = 4, 8, 2
MIB = 1024 * 1024


def mm(a, b):
    return jnp.dot(a, b, preferred_element_type=jnp.float32, precision=lax.Precision.HIGHEST)


def tiny_inverses(blocks):
    n = len(blocks)
    lane = lax.broadcasted_iota(jnp.int32, (16, 128), 1)
    row = lax.broadcasted_iota(jnp.int32, (16, 128), 0)
    seg = lane // 16
    packed = []
    for a in blocks:
        p = jnp.zeros((16, 128), jnp.float32)
        for s in range(8):
            p = jnp.where(seg == s, a[16 * s : 16 * s + 16, :], p)
        packed.append(p)
    p = jnp.concatenate(packed, axis=0)
    lane_n = lax.broadcasted_iota(jnp.int32, (16 * n, 128), 1)
    r = jnp.where(lane == seg * 16 + row, 1.0, 0.0).astype(jnp.float32)
    r = jnp.broadcast_to(r[None], (n, 16, 128))
    row3 = lax.broadcasted_iota(jnp.int32, (n, 16, 128), 1)
    for j in range(16):
        idx = (lane_n // 16) * 16 + j
        column = jnp.take_along_axis(p, idx, axis=1).reshape(n, 16, 128)
        w = r[:, j : j + 1, :] / column[:, j : j + 1, :]
        r = jnp.where(row3 > j, r - column * w, jnp.where(row3 == j, w, r))
    return [
        jnp.concatenate([jnp.where(seg == s, r[b], 0.0) for s in range(8)], axis=0) for b in range(n)
    ]


def grow(a, d, s):
    i = lax.broadcasted_iota(jnp.int32, a.shape, 0)
    k = lax.broadcasted_iota(jnp.int32, a.shape, 1)
    off = (i // (2 * s) == k // (2 * s)) & ((i // s) % 2 == 1) & ((k // s) % 2 == 0)
    return d - mm(d, mm(jnp.where(off, a, 0.0), d))


BELOW = ((1, 0), (2, 0), (2, 1), (3, 0), (3, 1), (3, 2))


def split(a):
    high = a.astype(jnp.bfloat16)
    return high, (a - high.astype(jnp.float32)).astype(jnp.bfloat16)


def prepare_kernel(where, *refs):
    own4, other4, (inverse_out, start_out, mark, diagonal, rhs, inverse, start, sems) = refs[:4], refs[4:8], refs[8:]
    for refs4, core in ((own4, where[0]), (other4, 1 - where[0])):
        for n in range(NY):
            plane = (where[1] + n) % NY
            diagonal[plane, :, core] = refs4[n][:, :, :256]
            rhs[plane, :, core] = refs4[n][:, :, 256:]
    whole = [diagonal[k].reshape(256, 256) for k in range(NY)]
    blocks = []
    for k in range(NY):
        blocks += [whole[k][:128, :128], whole[k][128:, 128:]]
    ds = tiny_inverses(blocks)
    for s in (16, 32, 64):
        ds = [grow(a, d, s) for a, d in zip(blocks, ds)]
    lows = [mm(ds[2 * k + 1], mm(whole[k][128:, :128], ds[2 * k])) for k in range(NY)]
    for k in range(NY):
        inverse[k, :128, :128] = ds[2 * k]
        inverse[k, :128, 128:] = jnp.zeros((128, 128), jnp.float32)
        inverse[k, 128:, :128] = -lows[k]
        inverse[k, 128:, 128:] = ds[2 * k + 1]
    copies_out = [
        [pltpu.make_async_copy(inverse.at[k], inverse_out.at[k - 1], sems.at[0, k]) for k in range(1, NY)],
        [pltpu.make_async_copy(start.at[k], start_out.at[k], sems.at[1, k]) for k in range(NY)],
    ]
    for copy in copies_out[0]:
        copy.start()
    for k in range(NY):
        start[k] = mm(inverse[k], rhs[k].reshape(256, 512))
        copies_out[1][k].start()
    mark[...] = start[NY - 1, :8, :128]
    for copy in copies_out[0] + copies_out[1]:
        copy.wait()


def prepare(where, own, other):
    vmem = pl.BlockSpec(memory_space=pltpu.VMEM)
    return pl.pallas_call(
        prepare_kernel,
        out_shape=[pltpu.HBM(s, jnp.float32) for s in ((NY - 1, 256, 256), (NY, 256, 512))]
        + [jax.ShapeDtypeStruct((8, 128), jnp.float32)],
        in_specs=[pl.BlockSpec(memory_space=pltpu.SMEM)] + [vmem] * 8,
        out_specs=[pl.BlockSpec(memory_space=pltpu.HBM)] * 2 + [vmem],
        scratch_shapes=[
            pltpu.VMEM((NY, NZ, NC, 16, 256), jnp.float32),
            pltpu.VMEM((NY, NZ, NC, 16, 512), jnp.float32),
            pltpu.VMEM((NY, 256, 256), jnp.float32),
            pltpu.VMEM((NY, 256, 512), jnp.float32),
            pltpu.SemaphoreType.DMA((2, NY)),
        ],
        compiler_params=pltpu.CompilerParams(vmem_limit_bytes=16 * MIB),
        cost_estimate=pl.CostEstimate(flops=10 * 10**9, bytes_accessed=8 * MIB, transcendentals=0),
    )(where, *own, *other)


def solve_kernel(where, low_own, low_other, inverse_in, start_in, mark, own, right, far, left, *refs):
    stripe, *outs, x_ref, lower, inverse, start, panel, sems, panel_sems = refs
    core, col = where[0], where[4]
    fetches = [[pltpu.make_async_copy(start_in.at[k], start.at[k], sems.at[0, k])] for k in range(NY)]
    for k in range(1, NY):
        fetches[k].append(pltpu.make_async_copy(inverse_in.at[k - 1], inverse.at[k - 1], sems.at[1, k]))
    for copy in fetches[0] + fetches[1]:
        copy.start()
    for n in range(len(BELOW)):
        lower[n, :, core] = low_own[:, n]
        lower[n, :, 1 - core] = low_other[:, n]
    for copy in fetches[0]:
        copy.wait()
    for shift, piece in enumerate((own, right, far, left)):
        k = (col + shift) % 4
        pltpu.make_async_copy(piece, panel.at[k], panel_sems.at[k]).start()
    for copy in fetches[2] + fetches[3]:
        copy.start()
    for k in range(NY + 1):
        if 0 < k < NY:
            for copy in fetches[k]:
                copy.wait()
        if k > 0:
            pltpu.make_async_copy(own, panel.at[k - 1], panel_sems.at[k - 1]).wait()
        if k < NY:
            rows = slice(256 * k, 256 * k + 256)
            x = start[k]
            if k > 0:
                total = jnp.zeros((256, 512), jnp.float32)
                for j in range(k):
                    n = BELOW.index((k, j))
                    total += mm(lower[n].reshape(256, 256), x_ref[256 * j : 256 * j + 256, :])
                x = x - mm(inverse[k - 1], total)
            x_ref[rows, :] = x
        if k > 0:
            for t in range(panel.shape[1] // 256):
                tile = slice(256 * t, 256 * t + 256)
                ah, al = split(panel[k - 1, tile, :])
                part = jnp.dot(ah, xh, preferred_element_type=jnp.float32)
                part += jnp.dot(ah, xl, preferred_element_type=jnp.float32)
                part += jnp.dot(al, xh, preferred_element_type=jnp.float32)
                for j in range(4):
                    piece = part[:, 128 * j : 128 * j + 128]
                    outs[j][tile, :] = piece if k == 1 else outs[j][tile, :] + piece
        if k < NY:
            turned = [x_ref[rows, pl.ds(pl.multiple_of((col + j) % 4 * 128, 128), 128)] for j in range(4)]
            xh, xl = split(jnp.concatenate(turned, axis=1))
    stripe[...] = x_ref[pl.ds(pl.multiple_of(where[2], 16), 16), pl.ds(pl.multiple_of(where[3], 128), 128)]


def solve_and_multiply(where, low_own, low_other, inverse, start, mark, pieces):
    vmem, anywhere = pl.BlockSpec(memory_space=pltpu.VMEM), pl.BlockSpec(memory_space=pl.ANY)
    n = pieces[0].shape[0]
    return pl.pallas_call(
        solve_kernel,
        out_shape=[jax.ShapeDtypeStruct((16, 128), jnp.float32)] + [jax.ShapeDtypeStruct((n, 128), jnp.float32)] * 4,
        in_specs=[pl.BlockSpec(memory_space=pltpu.SMEM), vmem, vmem, anywhere, anywhere, vmem] + [anywhere] * 4,
        out_specs=[vmem] * 5,
        scratch_shapes=[
            pltpu.VMEM((1024, 512), jnp.float32),
            pltpu.VMEM((len(BELOW), NZ, NC, 16, 256), jnp.float32),
            pltpu.VMEM((NY - 1, 256, 256), jnp.float32),
            pltpu.VMEM((NY, 256, 512), jnp.float32),
            pltpu.VMEM((4, n, 256), jnp.float32),
            pltpu.SemaphoreType.DMA((2, NY)),
            pltpu.SemaphoreType.DMA((4,)),
        ],
        compiler_params=pltpu.CompilerParams(vmem_limit_bytes=20 * MIB),
        cost_estimate=pl.CostEstimate(flops=8 * 10**9, bytes_accessed=8 * MIB, transcendentals=0),
    )(where, low_own, low_other, inverse, start, mark, *pieces)


def finish_kernel(sources, rhs, *refs):
    pieces, out = refs[: sources.shape[0]], refs[-1]
    for n, piece in enumerate(pieces):

        @pl.when(pl.program_id(0) == n)
        def _():
            out[...] = rhs[...] - piece[...]


def finish(sources, rhs, pieces, before):
    block = pl.BlockSpec(pieces[0].shape, lambda i, s: (s[i], 0))
    prior = [] if before is None else [before]
    return pl.pallas_call(
        finish_kernel,
        out_shape=jax.ShapeDtypeStruct(rhs.shape, jnp.float32),
        grid_spec=pltpu.PrefetchScalarGridSpec(
            num_scalar_prefetch=1,
            grid=(len(pieces),),
            in_specs=[block]
            + [pl.BlockSpec(p.shape, lambda i, s: (0, 0)) for p in pieces]
            + [pl.BlockSpec(memory_space=pl.ANY)] * len(prior),
            out_specs=block,
        ),
        input_output_aliases={2 + len(pieces): 0} if prior else {},
        compiler_params=pltpu.CompilerParams(vmem_limit_bytes=16 * MIB),
        cost_estimate=pl.CostEstimate(flops=rhs.size, bytes_accessed=3 * rhs.size, transcendentals=0),
    )(sources, rhs, *pieces, *prior)


def copies_kernel(fill, n, *refs):
    out = refs[-1]
    fill(*refs)
    for i in range(1, n):
        out[i] = out[0]


def copies(fill, n, shape, *args):
    vmem = pl.BlockSpec(memory_space=pltpu.VMEM)
    inputs = pl.BlockSpec() if fill is fill_mine else vmem
    specs = [pl.BlockSpec(memory_space=pltpu.SMEM) if a.dtype == jnp.int32 else inputs for a in args]
    return pl.pallas_call(
        functools.partial(copies_kernel, fill, n),
        out_shape=jax.ShapeDtypeStruct((n,) + shape, jnp.float32),
        in_specs=specs,
        out_specs=vmem,
        compiler_params=pltpu.CompilerParams(vmem_limit_bytes=8 * MIB),
        cost_estimate=pl.CostEstimate(flops=0, bytes_accessed=MIB, transcendentals=0),
    )(*args)


def fill_mine(diag, rhs, out):
    out[0, :, :256] = diag[...]
    out[0, :, 256:] = rhs[...]


def fill_rest(where, mine, out):
    out[0, :, :256] = mine[where[1], :, :256]
    for c in range(4):
        out[0, :, 256 + 128 * c : 384 + 128 * c] = mine[c, :, 256:]


def fill_low(where, mine, *refs):
    out = refs[3]
    for n, (k, j) in enumerate(BELOW):
        step = (k - where[1] + NY) % NY
        part = mine[j, :, :256]
        for m in range(3):
            part = jnp.where(step == m + 1, refs[m][j], part)
        out[0, n] = part


def z_groups():
    return [[(y * NZ + z) * NC + c for z in range(NZ)] for y in range(NY) for c in range(NC)]


def y_groups():
    return [[(y * NZ + z) * NC + c for y in range(NY)] for z in range(NZ) for c in range(NC)]


def send_copies(a, axis, groups=None):
    return lax.all_to_all(a, axis, 0, 0, tiled=True, axis_index_groups=groups)


def swap_cores(a):
    return lax.ppermute(a, "row", [(i, i ^ 1) for i in range(NY * NZ * NC)])


def shift_y(a, k):
    step = k * NZ * NC
    n = NY * NZ * NC
    return lax.ppermute(a, "row", [(i, (i + step) % n) for i in range(n)])


def send_x(a, k):
    return lax.ppermute(a, "col", [(i, (i + k) % 4) for i in range(4)])


def per_device(diag_block, block_rhs, panel, trailing_rhs):
    row, col = lax.axis_index("row"), lax.axis_index("col")
    y = row // (NZ * NC)
    where = jnp.stack([row % NC, y, row * 16, col * 128, col]).astype(jnp.int32)

    mine = send_copies(copies(fill_mine, 4, (16, 384), *[pltpu.with_memory_space_constraint(a, pltpu.HBM) for a in (diag_block, block_rhs)]), "col")
    quarter = panel.shape[0] // 4
    own, *pieces = [lax.dynamic_slice_in_dim(panel, (col + k) % 4 * quarter, quarter, 0) for k in (0, 2, 1, 3)]
    mine, pieces = lax.optimization_barrier((mine, pieces))
    far, left, right = [send_x(p, k) for k, p in zip((2, 1, 3), pieces)]

    rest = send_copies(copies(fill_rest, NZ, (16, 768), where, mine), "row", z_groups())
    lows = [shift_y(mine[:3, :, :256], k) for k in (3, 2, 1)]
    rest, lows = lax.optimization_barrier((rest, lows))
    low = send_copies(copies(fill_low, NZ, (6, 16, 256), where, mine, *lows), "row", z_groups())
    rests = [rest] + [shift_y(rest, k) for k in (3, 2, 1)]
    swapped = [swap_cores(r) for r in rests]
    far, left, right, swapped[0] = lax.optimization_barrier((far, left, right, swapped[0]))
    inverse, start, mark = prepare(where, rests, swapped)
    low, mark = lax.optimization_barrier((low, mark))
    inverse, start = [pltpu.with_memory_space_constraint(a, pltpu.HBM) for a in (inverse, start)]
    stripe, mine, to_right, to_far, to_left = solve_and_multiply(
        where, low, swap_cores(low), inverse, start, mark, (own, right, far, left)
    )

    got_left, got_right, got_far = send_x(to_right, 1), send_x(to_left, 3), send_x(to_far, 2)

    def sources(*shifts):
        return jnp.stack([(col + k) % 4 for k in shifts]).astype(jnp.int32)

    trailing = finish(sources(0), trailing_rhs, [mine], None)
    trailing = finish(sources(3, 1), trailing_rhs, [got_left, got_right], trailing)
    trailing = finish(sources(2), trailing_rhs, [got_far], trailing)
    return (stripe, trailing)


def solution(mesh):
    specs = (P("row", "col"),) * 4
    return jax.shard_map(per_device, mesh=mesh, in_specs=specs, out_specs=(P("row", "col"),) * 2, check_vma=False)
```

```python
import functools

import jax
import jax.numpy as jnp
from jax import lax
from jax.experimental import pallas as pl
from jax.experimental.pallas import tpu as pltpu
from jax.sharding import PartitionSpec as P

NY, NZ, NC = 4, 8, 2
MIB = 1024 * 1024


def mm(a, b):
    return jnp.dot(a, b, preferred_element_type=jnp.float32, precision=lax.Precision.HIGHEST)


def tiny_inverses(blocks):
    n = len(blocks)
    lane = lax.broadcasted_iota(jnp.int32, (16, 128), 1)
    row = lax.broadcasted_iota(jnp.int32, (16, 128), 0)
    seg = lane // 16
    packed = []
    for a in blocks:
        p = jnp.zeros((16, 128), jnp.float32)
        for s in range(8):
            p = jnp.where(seg == s, a[16 * s : 16 * s + 16, :], p)
        packed.append(p)
    p = jnp.concatenate(packed, axis=0)
    lane_n = lax.broadcasted_iota(jnp.int32, (16 * n, 128), 1)
    r = jnp.where(lane == seg * 16 + row, 1.0, 0.0).astype(jnp.float32)
    r = jnp.broadcast_to(r[None], (n, 16, 128))
    row3 = lax.broadcasted_iota(jnp.int32, (n, 16, 128), 1)
    for j in range(16):
        idx = (lane_n // 16) * 16 + j
        column = jnp.take_along_axis(p, idx, axis=1).reshape(n, 16, 128)
        w = r[:, j : j + 1, :] / column[:, j : j + 1, :]
        r = jnp.where(row3 > j, r - column * w, jnp.where(row3 == j, w, r))
    return [
        jnp.concatenate([jnp.where(seg == s, r[b], 0.0) for s in range(8)], axis=0) for b in range(n)
    ]


def grow(a, d, s):
    i = lax.broadcasted_iota(jnp.int32, a.shape, 0)
    k = lax.broadcasted_iota(jnp.int32, a.shape, 1)
    off = (i // (2 * s) == k // (2 * s)) & ((i // s) % 2 == 1) & ((k // s) % 2 == 0)
    return d - mm(d, mm(jnp.where(off, a, 0.0), d))


BELOW = ((1, 0), (2, 0), (2, 1), (3, 0), (3, 1), (3, 2))


def split(a):
    high = a.astype(jnp.bfloat16)
    return high, (a - high.astype(jnp.float32)).astype(jnp.bfloat16)


def prepare_kernel(where, *refs):
    own4, other4, (inverse_out, start_out, mark, diagonal, rhs, inverse, start, sems) = refs[:4], refs[4:8], refs[8:]
    for refs4, core in ((own4, where[0]), (other4, 1 - where[0])):
        for n in range(NY):
            plane = (where[1] + n) % NY
            diagonal[plane, :, core] = refs4[n][:, :, :256]
            rhs[plane, :, core] = refs4[n][:, :, 256:]
    whole = [diagonal[k].reshape(256, 256) for k in range(NY)]
    blocks = []
    for k in range(NY):
        blocks += [whole[k][:128, :128], whole[k][128:, 128:]]
    ds = tiny_inverses(blocks)
    for s in (16, 32, 64):
        ds = [grow(a, d, s) for a, d in zip(blocks, ds)]
    lows = [mm(ds[2 * k + 1], mm(whole[k][128:, :128], ds[2 * k])) for k in range(NY)]
    for k in range(NY):
        inverse[k, :128, :128] = ds[2 * k]
        inverse[k, :128, 128:] = jnp.zeros((128, 128), jnp.float32)
        inverse[k, 128:, :128] = -lows[k]
        inverse[k, 128:, 128:] = ds[2 * k + 1]
    copies_out = [
        [pltpu.make_async_copy(inverse.at[k], inverse_out.at[k - 1], sems.at[0, k]) for k in range(1, NY)],
        [pltpu.make_async_copy(start.at[k], start_out.at[k], sems.at[1, k]) for k in range(NY)],
    ]
    for copy in copies_out[0]:
        copy.start()
    for k in range(NY):
        start[k] = mm(inverse[k], rhs[k].reshape(256, 512))
        copies_out[1][k].start()
    mark[...] = start[NY - 1, :8, :128]
    for copy in copies_out[0] + copies_out[1]:
        copy.wait()


def prepare(where, own, other):
    vmem = pl.BlockSpec(memory_space=pltpu.VMEM)
    return pl.pallas_call(
        prepare_kernel,
        out_shape=[pltpu.HBM(s, jnp.float32) for s in ((NY - 1, 256, 256), (NY, 256, 512))]
        + [jax.ShapeDtypeStruct((8, 128), jnp.float32)],
        in_specs=[pl.BlockSpec(memory_space=pltpu.SMEM)] + [vmem] * 8,
        out_specs=[pl.BlockSpec(memory_space=pltpu.HBM)] * 2 + [vmem],
        scratch_shapes=[
            pltpu.VMEM((NY, NZ, NC, 16, 256), jnp.float32),
            pltpu.VMEM((NY, NZ, NC, 16, 512), jnp.float32),
            pltpu.VMEM((NY, 256, 256), jnp.float32),
            pltpu.VMEM((NY, 256, 512), jnp.float32),
            pltpu.SemaphoreType.DMA((2, NY)),
        ],
        compiler_params=pltpu.CompilerParams(vmem_limit_bytes=16 * MIB),
        cost_estimate=pl.CostEstimate(flops=10 * 10**9, bytes_accessed=8 * MIB, transcendentals=0),
    )(where, *own, *other)


TAKE = ((), (), (), (0, 1, 2), (3,))


def solve_kernel(where, low_own, low_other, inverse_in, start_in, mark, own, right, far, left, *refs):
    stripe, *outs, x_ref, lower, inverse, start, panel, sems, panel_sems = refs
    core, col = where[0], where[4]
    fetches = [[pltpu.make_async_copy(start_in.at[k], start.at[k], sems.at[0, k])] for k in range(NY)]
    for k in range(1, NY):
        fetches[k].append(pltpu.make_async_copy(inverse_in.at[k - 1], inverse.at[k - 1], sems.at[1, k]))
    for copy in fetches[0] + fetches[1]:
        copy.start()
    for n in range(len(BELOW)):
        lower[n, :, core] = low_own[:, n]
        lower[n, :, 1 - core] = low_other[:, n]
    for copy in fetches[0]:
        copy.wait()
    for shift, piece in enumerate((own, right, far, left)):
        k = (col + shift) % 4
        pltpu.make_async_copy(piece, panel.at[k], panel_sems.at[k]).start()
    for copy in fetches[2] + fetches[3]:
        copy.start()
    halves = []
    for k in range(NY + 1):
        if 0 < k < NY:
            for copy in fetches[k]:
                copy.wait()
        for j in TAKE[k]:
            pltpu.make_async_copy(own, panel.at[j], panel_sems.at[j]).wait()
        if k < NY:
            rows = slice(256 * k, 256 * k + 256)
            x = start[k]
            if k > 0:
                total = jnp.zeros((256, 512), jnp.float32)
                for j in range(k):
                    n = BELOW.index((k, j))
                    total += mm(lower[n].reshape(256, 256), x_ref[256 * j : 256 * j + 256, :])
                x = x - mm(inverse[k - 1], total)
            x_ref[rows, :] = x
        if TAKE[k]:
            high, low = [jnp.concatenate([x[n] for x in halves[TAKE[k][0] :]], axis=0) for n in range(2)]
            for t in range(panel.shape[1] // 256):
                tile = slice(256 * t, 256 * t + 256)
                ah, al = split(jnp.concatenate([panel[j, tile, :] for j in TAKE[k]], axis=1))
                part = jnp.dot(ah, high, preferred_element_type=jnp.float32)
                part += jnp.dot(ah, low, preferred_element_type=jnp.float32)
                part += jnp.dot(al, high, preferred_element_type=jnp.float32)
                for j in range(4):
                    piece = part[:, 128 * j : 128 * j + 128]
                    outs[j][tile, :] = piece if TAKE[k][0] == 0 else outs[j][tile, :] + piece
        if k < NY:
            turned = [x_ref[rows, pl.ds(pl.multiple_of((col + j) % 4 * 128, 128), 128)] for j in range(4)]
            halves.append(split(jnp.concatenate(turned, axis=1)))
    stripe[...] = x_ref[pl.ds(pl.multiple_of(where[2], 16), 16), pl.ds(pl.multiple_of(where[3], 128), 128)]


def solve_and_multiply(where, low_own, low_other, inverse, start, mark, pieces):
    vmem, anywhere = pl.BlockSpec(memory_space=pltpu.VMEM), pl.BlockSpec(memory_space=pl.ANY)
    n = pieces[0].shape[0]
    return pl.pallas_call(
        solve_kernel,
        out_shape=[jax.ShapeDtypeStruct((16, 128), jnp.float32)] + [jax.ShapeDtypeStruct((n, 128), jnp.float32)] * 4,
        in_specs=[pl.BlockSpec(memory_space=pltpu.SMEM), vmem, vmem, anywhere, anywhere, vmem] + [anywhere] * 4,
        out_specs=[vmem] * 5,
        scratch_shapes=[
            pltpu.VMEM((1024, 512), jnp.float32),
            pltpu.VMEM((len(BELOW), NZ, NC, 16, 256), jnp.float32),
            pltpu.VMEM((NY - 1, 256, 256), jnp.float32),
            pltpu.VMEM((NY, 256, 512), jnp.float32),
            pltpu.VMEM((4, n, 256), jnp.float32),
            pltpu.SemaphoreType.DMA((2, NY)),
            pltpu.SemaphoreType.DMA((4,)),
        ],
        compiler_params=pltpu.CompilerParams(vmem_limit_bytes=20 * MIB),
        cost_estimate=pl.CostEstimate(flops=8 * 10**9, bytes_accessed=8 * MIB, transcendentals=0),
    )(where, low_own, low_other, inverse, start, mark, *pieces)


def finish_kernel(sources, rhs, *refs):
    pieces, out = refs[: sources.shape[0]], refs[-1]
    for n, piece in enumerate(pieces):

        @pl.when(pl.program_id(0) == n)
        def _():
            out[...] = rhs[...] - piece[...]


def finish(sources, rhs, pieces, before):
    block = pl.BlockSpec(pieces[0].shape, lambda i, s: (s[i], 0))
    prior = [] if before is None else [before]
    return pl.pallas_call(
        finish_kernel,
        out_shape=jax.ShapeDtypeStruct(rhs.shape, jnp.float32),
        grid_spec=pltpu.PrefetchScalarGridSpec(
            num_scalar_prefetch=1,
            grid=(len(pieces),),
            in_specs=[block]
            + [pl.BlockSpec(p.shape, lambda i, s: (0, 0)) for p in pieces]
            + [pl.BlockSpec(memory_space=pl.ANY)] * len(prior),
            out_specs=block,
        ),
        input_output_aliases={2 + len(pieces): 0} if prior else {},
        compiler_params=pltpu.CompilerParams(vmem_limit_bytes=16 * MIB),
        cost_estimate=pl.CostEstimate(flops=rhs.size, bytes_accessed=3 * rhs.size, transcendentals=0),
    )(sources, rhs, *pieces, *prior)


def copies_kernel(fill, n, *refs):
    out = refs[-1]
    fill(*refs)
    for i in range(1, n):
        out[i] = out[0]


def copies(fill, n, shape, *args):
    vmem = pl.BlockSpec(memory_space=pltpu.VMEM)
    inputs = pl.BlockSpec() if fill is fill_mine else vmem
    specs = [pl.BlockSpec(memory_space=pltpu.SMEM) if a.dtype == jnp.int32 else inputs for a in args]
    return pl.pallas_call(
        functools.partial(copies_kernel, fill, n),
        out_shape=jax.ShapeDtypeStruct((n,) + shape, jnp.float32),
        in_specs=specs,
        out_specs=vmem,
        compiler_params=pltpu.CompilerParams(vmem_limit_bytes=8 * MIB),
        cost_estimate=pl.CostEstimate(flops=0, bytes_accessed=MIB, transcendentals=0),
    )(*args)


def fill_mine(diag, rhs, out):
    out[0, :, :256] = diag[...]
    out[0, :, 256:] = rhs[...]


def fill_rest(where, mine, out):
    out[0, :, :256] = mine[where[1], :, :256]
    for c in range(4):
        out[0, :, 256 + 128 * c : 384 + 128 * c] = mine[c, :, 256:]


def fill_low(where, mine, *refs):
    out = refs[3]
    for n, (k, j) in enumerate(BELOW):
        step = (k - where[1] + NY) % NY
        part = mine[j, :, :256]
        for m in range(3):
            part = jnp.where(step == m + 1, refs[m][j], part)
        out[0, n] = part


def z_groups():
    return [[(y * NZ + z) * NC + c for z in range(NZ)] for y in range(NY) for c in range(NC)]


def y_groups():
    return [[(y * NZ + z) * NC + c for y in range(NY)] for z in range(NZ) for c in range(NC)]


def send_copies(a, axis, groups=None):
    return lax.all_to_all(a, axis, 0, 0, tiled=True, axis_index_groups=groups)


def swap_cores(a):
    return lax.ppermute(a, "row", [(i, i ^ 1) for i in range(NY * NZ * NC)])


def shift_y(a, k):
    step = k * NZ * NC
    n = NY * NZ * NC
    return lax.ppermute(a, "row", [(i, (i + step) % n) for i in range(n)])


def send_x(a, k):
    return lax.ppermute(a, "col", [(i, (i + k) % 4) for i in range(4)])


def per_device(diag_block, block_rhs, panel, trailing_rhs):
    row, col = lax.axis_index("row"), lax.axis_index("col")
    y = row // (NZ * NC)
    where = jnp.stack([row % NC, y, row * 16, col * 128, col]).astype(jnp.int32)

    mine = send_copies(copies(fill_mine, 4, (16, 384), *[pltpu.with_memory_space_constraint(a, pltpu.HBM) for a in (diag_block, block_rhs)]), "col")
    quarter = panel.shape[0] // 4
    own, *pieces = [lax.dynamic_slice_in_dim(panel, (col + k) % 4 * quarter, quarter, 0) for k in (0, 2, 1, 3)]
    mine, pieces = lax.optimization_barrier((mine, pieces))
    far, left, right = [send_x(p, k) for k, p in zip((2, 1, 3), pieces)]

    rest = send_copies(copies(fill_rest, NZ, (16, 768), where, mine), "row", z_groups())
    lows = [shift_y(mine[:3, :, :256], k) for k in (3, 2, 1)]
    rest, lows = lax.optimization_barrier((rest, lows))
    low = send_copies(copies(fill_low, NZ, (6, 16, 256), where, mine, *lows), "row", z_groups())
    rests = [rest] + [shift_y(rest, k) for k in (3, 2, 1)]
    swapped = [swap_cores(r) for r in rests]
    far, left, right, swapped[0] = lax.optimization_barrier((far, left, right, swapped[0]))
    inverse, start, mark = prepare(where, rests, swapped)
    low, mark = lax.optimization_barrier((low, mark))
    inverse, start = [pltpu.with_memory_space_constraint(a, pltpu.HBM) for a in (inverse, start)]
    stripe, mine, to_right, to_far, to_left = solve_and_multiply(
        where, low, swap_cores(low), inverse, start, mark, (own, right, far, left)
    )

    got_left, got_right, got_far = send_x(to_right, 1), send_x(to_left, 3), send_x(to_far, 2)

    def sources(*shifts):
        return jnp.stack([(col + k) % 4 for k in shifts]).astype(jnp.int32)

    trailing = finish(sources(0), trailing_rhs, [mine], None)
    trailing = finish(sources(3, 1), trailing_rhs, [got_left, got_right], trailing)
    trailing = finish(sources(2), trailing_rhs, [got_far], trailing)
    return (stripe, trailing)


def solution(mesh):
    specs = (P("row", "col"),) * 4
    return jax.shard_map(per_device, mesh=mesh, in_specs=specs, out_specs=(P("row", "col"),) * 2, check_vma=False)
```
